32 devices in a mesh: parts: 2 (over x), trade: 16 (over z, y, core).
Axes of the slice: x: 2, y: 2, z: 4, core: 2. Of those that a mesh axis runs over, the one named last changes fastest.
Arguments:
- panels: bfloat16 [2, 256, 4096], P(None, 'parts', 'trade'), parts along dimension 1, may hold values from -6 to 6
- lin_weight: bfloat16 [1024, 4, 128, 128], P(('parts', 'trade')), parts along dimension 0, may hold values from -0.25 to 0.25
- quad_weight: bfloat16 [1024, 4, 128, 128], P(('parts', 'trade')), parts along dimension 0, may hold values from -0.25 to 0.25
- positions: float32 [1024, 128], P(('parts', 'trade')), parts along dimension 0, may hold values from -6 to 6
- pattern: int32 [1024, 4], P(('parts', 'trade')), parts along dimension 0, may hold values from 0 to 31, all different within a row
- netting: int32 [1024], P(('parts', 'trade')), parts along dimension 0, may hold values from 0 to 127
- default_curve: float32 [100], replicated, may hold values from 0.5 to 2
- date_ids: int32 [2], replicated, may hold values from 0 to 99
- loss_given: float32 [256], P('parts'), parts along dimension 0, may hold values from 0.3 to 0.9
Outputs:
- charge: float32 [4], P('parts'), parts along dimension 0
- panel_grad: float32 [2, 256, 4096], P(None, 'parts', 'trade'), parts along dimension 1
The draws below stay inside these ranges and needn't reach their ends.
There are 2 independent parts, one for each index of `parts`. The reference program is written for one: setup_inputs(seed, part) draws one part's arguments, and reference() takes and returns one part's arrays. A program takes and returns all parts, laid end to end along the dimension named above; an argument that names none is the same for every part. Nothing has to cross between parts.
Inputs may be any that keep to these rules, and one draw needn't show every extreme that they name: `pattern`: the 4 factor blocks of a trade block are distinct; every factor block is used by some trade block.
All inputs are finite; a program needn't handle non-finite values.
Results may differ from the reference program's by a relative error of at most 0.0029.
Values may be sent and summed in bfloat16 or wider, within the bound.
A program may use at most 128 MiB of HBM per device.

```python
import math
import jax
import jax.numpy as jnp
from jax import lax

FACTORS = 4096
BLOCK = 128
PICKS = 4
NETS = 128
DATES = 2
HORIZON = 100
SCEN = 128
TBLK = 512
TRADES = 65536


def touch_ends(array, own_key, smallest, high):
    extent = array.shape
    place = [jax.random.randint(jax.random.fold_in(own_key, axis), (), 0, extent[axis]) for axis in range(len(extent))]
    array = array.at[tuple(place)].set(smallest)
    longest = extent.index(max(extent))
    place[longest] = (place[longest] + 1) % extent[longest]
    return array.at[tuple(place)].set(high)


def steps_of(stream_key, dims, cuts, smallest, largest):
    level, own = 1.0, jax.random.fold_in(stream_key, 6)
    for dim, parts in cuts:
        heights = jnp.exp(jax.random.uniform(jax.random.fold_in(own, dim), (parts,), jnp.float32, smallest / len(cuts), largest / len(cuts)))
        level = level * jnp.repeat(heights, dims[dim] // parts).reshape([-1 if axis == dim else 1 for axis in range(len(dims))])
    return level


def different_ones(stream_key, rows, count, top, lift):
    sequence = jax.random.permutation(jax.random.fold_in(stream_key, 1), count)
    pull = sequence
    for power in range(3):
        pull = pull * pull // count
    pull = pull * lift // count
    chance = jax.random.randint(jax.random.fold_in(stream_key, 2), (rows, count), 0, 4096) + pull
    fixed_rows = jax.random.permutation(jax.random.fold_in(stream_key, 3), rows)[jnp.arange(count) % rows]
    chance = jnp.where(jnp.arange(rows)[:, None] == fixed_rows[None, :], 1 << 14, chance)
    score = chance * count + jnp.arange(count)
    return lax.top_k(score.astype(jnp.int32), top)[1].astype(jnp.int32)


def bell_draw(key, shape, scale, bound, split=(), held_as=jnp.bfloat16):
    drawn = jax.random.normal(key, shape, jnp.float32) * scale
    if len(split) > 0:
        drawn = steps_of(key, shape, split, -0.22, 0.18) * drawn
    return jnp.clip(drawn, min=-bound, max=bound).astype(held_as)


def setup_inputs(seed: int = 0, part: int = 0) -> dict:
    arg_keys = jax.random.split(jax.random.key(seed), 10)
    part_splits = jax.random.split(jax.random.fold_in(arg_keys[9], part), 10)
    return {
        "panels": bell_draw(part_splits[0], (DATES, SCEN, FACTORS), 1.0, 6.0, ((2, 16),)),
        "lin_weight": bell_draw(part_splits[1], (TBLK, PICKS, BLOCK, BLOCK), (PICKS * BLOCK) ** -0.5, 0.25, ((0, 16),)),
        "quad_weight": bell_draw(part_splits[2], (TBLK, PICKS, BLOCK, BLOCK), (PICKS * BLOCK) ** -0.5, 0.25, ((0, 16),)),
        "positions": bell_draw(part_splits[3], (TBLK, BLOCK), 1.0, 6.0, ((0, 16),), jnp.float32),
        "pattern": different_ones(part_splits[4], TBLK, FACTORS // BLOCK, PICKS, 2048),
        "netting": touch_ends(jax.random.randint(part_splits[5], (TBLK,), 0, NETS), jax.random.fold_in(part_splits[5], 1), 0, NETS - 1).astype(jnp.int32),
        "default_curve": jnp.clip(jnp.exp(jax.random.uniform(arg_keys[6], (HORIZON,), jnp.float32, math.log(0.5), math.log(2.0))), 0.5, 2.0),
        "date_ids": jax.random.randint(arg_keys[7], (DATES,), 0, HORIZON).astype(jnp.int32),
        "loss_given": jnp.clip(jax.random.uniform(part_splits[8], (NETS,), jnp.float32, 0.3, 0.9), 0.3, 0.9),
    }


def trade_terms(picked, lin_block, quad_block):
    linear = jnp.einsum('dsbkc,bkct->dsbt', picked.astype(jnp.float32), lin_block.astype(jnp.float32))
    square_term = jnp.einsum('dsbkc,bkct->dsbt', picked.astype(jnp.float32), quad_block.astype(jnp.float32))
    return linear, square_term


def reference(panels, lin_weight, quad_weight, positions, pattern, netting, default_curve, date_ids, loss_given):
    group_size = 8
    group_count = TBLK // group_size
    norm_scale = (NETS / TRADES) ** 0.5
    grad_unit = 1.0 / norm_scale
    fblocks = FACTORS // BLOCK
    weights = default_curve[date_ids]
    blocks = panels.reshape(DATES, SCEN, fblocks, BLOCK)
    set_ids = jnp.arange(NETS, dtype=jnp.int32)
    block_ids = jnp.arange(fblocks, dtype=jnp.int32)
    stacked = (lin_weight.reshape(group_count, group_size, PICKS, BLOCK, BLOCK),
               quad_weight.reshape(group_count, group_size, PICKS, BLOCK, BLOCK),
               positions.reshape(group_count, group_size, BLOCK),
               pattern.reshape(group_count, group_size * PICKS),
               netting.reshape(group_count, group_size))

    def evaluate(operands):
        lin_block, quad_block, position, pattern_rows, netting_rows = operands
        picked = jnp.take(blocks, pattern_rows, axis=2).reshape(DATES, SCEN, group_size, PICKS, BLOCK)
        linear, square_term = trade_terms(picked, lin_block, quad_block)
        trade_state = linear + 0.25 * square_term * square_term
        set_map = (netting_rows[:, None] == set_ids[None, :]).astype(jnp.float32)
        return square_term, trade_state, set_map

    def forward_step(running, operands):
        square_term, trade_state, set_map = evaluate(operands)
        block_sum = jnp.sum(operands[2][None, None] * jax.nn.softplus(trade_state), axis=-1)
        added = norm_scale * jnp.einsum('dsb,bn->dsn', block_sum, set_map, precision=lax.Precision.HIGHEST)
        return running + added, None

    exposure, _ = lax.scan(forward_step, jnp.zeros((DATES, SCEN, NETS), jnp.float32), stacked)
    losses = jnp.sum(loss_given * jax.nn.softplus(exposure), axis=-1)
    charge = weights * jnp.mean(losses, axis=-1)
    exposure_grad = weights[:, None, None] * loss_given * jax.nn.sigmoid(exposure)

    def backward_step(running, operands):
        square_term, trade_state, set_map = evaluate(operands)
        block_adjoint = norm_scale * jnp.einsum('dsn,bn->dsb', exposure_grad, set_map, precision=lax.Precision.HIGHEST)
        state_adjoint = block_adjoint[..., None] * operands[2][None, None] * jax.nn.sigmoid(trade_state)
        adjoint_lin = state_adjoint.astype(jnp.bfloat16)
        adjoint_square = (0.5 * square_term * state_adjoint).astype(jnp.bfloat16)
        contrib = jnp.einsum('dsbt,bkct->dsbkc', adjoint_lin.astype(jnp.float32), operands[0].astype(jnp.float32))
        contrib = contrib + jnp.einsum('dsbt,bkct->dsbkc', adjoint_square.astype(jnp.float32), operands[1].astype(jnp.float32))
        block_map = (operands[3][:, None] == block_ids[None, :]).astype(jnp.float32)
        placed = jnp.einsum('dsjc,jf->dsfc', contrib.reshape(DATES, SCEN, group_size * PICKS, BLOCK), block_map, precision=lax.Precision.HIGHEST)
        return running + grad_unit * placed, None

    gradient, _ = lax.scan(backward_step, jnp.zeros((DATES, SCEN, fblocks, BLOCK), jnp.float32), stacked)
    return charge, gradient.reshape(DATES, SCEN, FACTORS)
```

```python
import functools

import jax
import jax.numpy as jnp
from jax import lax
from jax.experimental import pallas as pl
from jax.experimental.pallas import tpu as pltpu
from jax.sharding import PartitionSpec as P

PICKS = 4
NETS = 128


def per_device(
    panels,
    lin_weight,
    quad_weight,
    positions,
    pattern,
    netting,
    default_curve,
    date_ids,
    loss_given,
):
    devices = lax.axis_size("trade")
    local_blocks, block_width = positions.shape
    trades_all = local_blocks * block_width * devices
    norm_scale = (NETS / trades_all) ** 0.5
    grad_unit = 1.0 / norm_scale
    factors = panels.shape[2] * devices
    fblocks = factors // block_width
    horizon = jnp.arange(default_curve.shape[0], dtype=jnp.int32)
    weights = jnp.sum(
        jnp.where(date_ids[:, None] == horizon[None, :], default_curve[None, :], 0.0), axis=1
    )
    set_map = (netting[:, None] == jnp.arange(NETS, dtype=jnp.int32)[None, :]).astype(jnp.float32)
    flat_pattern = pattern.reshape(-1)
    block_map = (flat_pattern[:, None] == jnp.arange(fblocks, dtype=jnp.int32)[None, :]).astype(
        jnp.float32
    )
    gathered = lax.all_gather(panels, "trade", axis=2, tiled=True)
    leading = gathered.shape[:-1]
    blocks = gathered.reshape(leading + (fblocks, block_width))
    picked = jnp.take(blocks, flat_pattern, axis=-2).reshape(
        leading + (local_blocks, PICKS, block_width)
    )
    linear = jnp.einsum(
        "...bkc,bkct->...bt", picked, lin_weight, preferred_element_type=jnp.float32
    )
    square_term = jnp.einsum(
        "...bkc,bkct->...bt", picked, quad_weight, preferred_element_type=jnp.float32
    )
    trade_state = linear + 0.25 * square_term * square_term
    block_sum = jnp.sum(positions * jax.nn.softplus(trade_state), axis=-1)
    local_exposure = norm_scale * jnp.einsum(
        "...b,bn->...n", block_sum, set_map, precision=lax.Precision.HIGHEST
    )
    local_exposure, square_term, trade_state = (local_exposure, square_term, trade_state)
    exposure = lax.psum(local_exposure, "trade")
    losses = jnp.sum(loss_given * jax.nn.softplus(exposure), axis=-1)
    charge = weights * jnp.mean(losses, axis=-1)
    exposure_grad = weights[:, None, None] * loss_given * jax.nn.sigmoid(exposure)
    block_adjoint = norm_scale * jnp.einsum(
        "...n,bn->...b", exposure_grad, set_map, precision=lax.Precision.HIGHEST
    )
    state_adjoint = block_adjoint[..., None] * positions * jax.nn.sigmoid(trade_state)
    adjoint_lin = state_adjoint.astype(jnp.bfloat16)
    adjoint_square = (0.5 * square_term * state_adjoint).astype(jnp.bfloat16)
    contrib = jnp.einsum(
        "...bt,bkct->...bkc", adjoint_lin, lin_weight, preferred_element_type=jnp.float32
    )
    contrib = contrib + jnp.einsum(
        "...bt,bkct->...bkc", adjoint_square, quad_weight, preferred_element_type=jnp.float32
    )
    leading = contrib.shape[:-3]
    flat_contrib = contrib.reshape(leading + (local_blocks * PICKS, block_width))
    leading = flat_contrib.shape[:-2]
    placed = jnp.einsum("...jc,jf->...fc", flat_contrib, block_map, precision=lax.Precision.HIGHEST)
    panel_grad = lax.psum_scatter(
        (grad_unit * placed).reshape(leading + (factors,)), "trade", scatter_dimension=2, tiled=True
    )
    return (charge, panel_grad)


MESH = pl.DeviceIdType.MESH
LANES = 128
CORES = 2
ROWS = 2
TRANSPOSED = (((1,), (1,)), ((), ()))


def fused_kernel(
    size,
    line,
    norm_scale,
    order_ref,
    last_ref,
    pattern_ref,
    netting_ref,
    dates_ref,
    curve_ref,
    keep_ref,
    used_ref,
    panels_ref,
    positions_ref,
    loss_ref,
    lin_hbm,
    quad_hbm,
    charge_ref,
    grad_ref,
    lin,
    quad,
    panels_a,
    panels_b,
    slope,
    half_square,
    exposure_part,
    exposure_pieces,
    exposure_full,
    contrib,
    running,
    core_out,
    core_in,
    kept,
    row_out,
    row_in,
    line_out,
    line_in,
    weight_sem,
    gather_send,
    gather_recv,
    piece_send,
    piece_recv,
    full_send,
    full_recv,
    core_send,
    core_recv,
    row_send,
    row_recv,
    line_send,
    line_recv,
):
    me = lax.axis_index("trade")
    core = lax.rem(me, CORES)
    row = lax.rem(me // CORES, ROWS)
    place = me // (CORES * ROWS)
    blocks = positions_ref.shape[0]
    scen = panels_ref.shape[1]
    own = panels_ref.shape[2] // LANES
    piece = scen // size
    gathered = (panels_a, panels_b)
    dates = len(gathered)

    def index(z, y, c):
        return (z * ROWS + y) * CORES + c

    def along(i):
        return lax.rem(place + i, line)

    def copy(src, dst, send, recv, peer):
        return pltpu.make_async_remote_copy(
            src_ref=src, dst_ref=dst, send_sem=send, recv_sem=recv,
            device_id={"trade": peer}, device_id_type=MESH,
        )

    row_peer = index(place, 1 - row, core)
    core_peer = index(place, row, 1 - core)

    weight_copies = [
        pltpu.make_async_copy(lin_hbm, lin, weight_sem.at[0]),
        pltpu.make_async_copy(quad_hbm, quad, weight_sem.at[1]),
    ]
    for each in weight_copies:
        each.start()

    for d in range(dates):
        for h in range(own):
            gathered[d][me * own + h] = panels_ref[d, :, h * LANES : (h + 1) * LANES]

    barrier = pltpu.get_barrier_semaphore()

    @pl.loop(1, size)
    def _(i):
        pl.semaphore_signal(
            barrier, inc=1, device_id={"trade": lax.rem(me + i, size)}, device_id_type=MESH
        )

    pl.semaphore_wait(barrier, size - 1)

    def panel_copy(d, slot, peer, k):
        part = gathered[d].at[pl.ds(slot * own, own)]
        return copy(part, part, gather_send.at[d, k], gather_recv.at[d, slot], peer)

    def forward_to_row(d, i):
        panel_copy(d, index(along(i), row, core), row_peer, line + i).start()

    def forward_to_core(d, i, y, k):
        panel_copy(d, index(along(i), y, core), core_peer, k).start()

    def panel_wait(d, slot):
        panel_copy(d, slot, core_peer, 0).wait_recv()

    def line_step(d, i):
        panel_wait(d, index(along(i), row, core))
        forward_to_row(d, i)
        forward_to_core(d, i, row, 2 * line + i)

    def row_step(d, i):
        panel_wait(d, index(along(i), 1 - row, core))
        forward_to_core(d, i, 1 - row, 3 * line + i)

    def core_steps(d):
        for i in range(line):
            for y in range(ROWS):
                panel_wait(d, index(along(i), y, 1 - core))

    def own_sends(d):
        forward_to_row(d, 0)
        forward_to_core(d, 0, row, 2 * line)

    def line_sends(d):
        for i in range(1, line):
            panel_copy(d, me, index(along(i), row, core), i).start()

    line_sends(0)
    own_sends(0)
    line_sends(1)
    for i in range(1, line):
        line_step(0, i)
    own_sends(1)
    for i in range(line):
        row_step(0, i)
    core_steps(0)
    for each in weight_copies:
        each.wait()

    lane = lax.broadcasted_iota(jnp.int32, (1, LANES), 1)

    def forward(d, first, stop):
        @pl.loop(first, stop)
        def _(b):
            picked = jnp.concatenate(
                [gathered[d][pattern_ref[b * PICKS + k]] for k in range(PICKS)], axis=1
            )
            both = jnp.concatenate([lin[b], quad[b]], axis=1)
            terms = jnp.dot(picked, both, preferred_element_type=jnp.float32)
            square = terms[:, LANES:]
            state = terms[:, :LANES] + 0.25 * square * square
            small = jnp.exp(-jnp.abs(state))
            above = 1.0 + small
            soft = jnp.maximum(state, 0.0) + jnp.log(above)
            sigmoid = jnp.where(state >= 0.0, 1.0, small) / above
            held = positions_ref[pl.ds(b, 1), :]
            block_sum = jnp.sum(held * soft, axis=1, keepdims=True)
            in_set = jnp.where(lane == netting_ref[b], norm_scale, 0.0)
            exposure_part[d] += block_sum * in_set
            slope[d, b] = held * sigmoid
            half_square[d, b] = 0.5 * square

    def piece_rows(t):
        return pl.ds(pl.multiple_of(t * piece, piece), piece)

    def piece_copy(d, t, source):
        return copy(
            exposure_part.at[d, piece_rows(t)], exposure_pieces.at[d, source],
            piece_send.at[d, t], piece_recv.at[d, source], t,
        )

    def full_copy(d, t, source):
        return copy(
            exposure_full.at[d, piece_rows(source)], exposure_full.at[d, piece_rows(source)],
            full_send.at[d, t], full_recv.at[d, source], t,
        )

    def others(act):
        @pl.loop(1, size)
        def _(i):
            act(lax.rem(me + i, size))

    def exposure_send(d):
        exposure_pieces[d, me] = exposure_part[d, piece_rows(me), :]
        others(lambda t: piece_copy(d, t, me).start())

    def exposure_sum(d):
        others(lambda t: piece_copy(d, t, t).wait_recv())
        exposure_full[d, piece_rows(me), :] = jnp.sum(exposure_pieces[d], axis=0)
        others(lambda t: full_copy(d, t, me).start())

    def exposure_grad(d):
        others(lambda t: full_copy(d, t, t).wait_recv())
        exposure = exposure_full[d]
        small = jnp.exp(-jnp.abs(exposure))
        above = 1.0 + small
        loss = loss_ref[...]
        weight = curve_ref[dates_ref[d]]
        soft = jnp.maximum(exposure, 0.0) + jnp.log(above)
        charge_ref[d] = weight * (jnp.sum(loss * soft) * (1.0 / scen))
        return weight * loss * (jnp.where(exposure >= 0.0, 1.0, small) / above)

    def backward(d, grad, first, stop):
        @pl.loop(first, stop)
        def _(b):
            in_set = jnp.where(lane == netting_ref[b], norm_scale, 0.0)
            adjoint = jnp.sum(grad * in_set, axis=1, keepdims=True) * slope[d, b]
            sent = jnp.concatenate(
                [
                    adjoint.astype(jnp.bfloat16),
                    (half_square[d, b] * adjoint).astype(jnp.bfloat16),
                ],
                axis=1,
            )
            both = jnp.concatenate([lin[b], quad[b]], axis=1)
            out = lax.dot_general(sent, both, TRANSPOSED, preferred_element_type=jnp.float32)
            for k in range(PICKS):
                contrib[b * PICKS + k] = out[:, k * LANES : (k + 1) * LANES]

    def add_up():
        running[0] = contrib[order_ref[0]]

        @pl.loop(1, blocks * PICKS)
        def _(j):
            running[j] = contrib[order_ref[j]] + keep_ref[j] * running[j - 1]

    def total(slot, h):
        p = slot * own + h
        return running[last_ref[p]] * used_ref[p]

    def core_copy(d, y, z):
        at = d, y * line + z
        return copy(core_out.at[at], core_in.at[at], core_send.at[at], core_recv.at[at], core_peer)

    def row_copy(d, z):
        at = d, z
        return copy(row_out.at[at], row_in.at[at], row_send.at[at], row_recv.at[at], row_peer)

    def line_copy(d, i, here, there):
        return copy(
            line_out.at[d, i], line_in.at[d, here], line_send.at[d, i], line_recv.at[d, here],
            index(there, row, core),
        )

    def core_stage(d):
        for y in (1 - row, row):
            @pl.loop(0, line)
            def _(z):
                for h in range(own):
                    core_out[d, y * line + z, h] = total(index(z, y, 1 - core), h).astype(
                        jnp.bfloat16
                    )
                core_copy(d, y, z).start()

        for y in (1 - row, row):
            @pl.loop(0, line)
            def _(z):
                for h in range(own):
                    kept[d, y * line + z, h] = total(index(z, y, core), h)

    def row_stage(d):
        @pl.loop(0, line)
        def _(z):
            core_copy(d, 1 - row, z).wait_recv()
            at = (1 - row) * line + z
            row_out[d, z] = (kept[d, at] + core_in[d, at].astype(jnp.float32)).astype(jnp.bfloat16)
            row_copy(d, z).start()

    def chip_sum(d, z):
        core_copy(d, row, z).wait_recv()
        row_copy(d, z).wait_recv()
        at = row * line + z
        return (
            kept[d, at]
            + core_in[d, at].astype(jnp.float32)
            + row_in[d, z].astype(jnp.float32)
        )

    def line_stage(d):
        for i in range(1, line):
            there = along(i)
            line_out[d, i] = chip_sum(d, there).astype(jnp.bfloat16)
            line_copy(d, i, place, there).start()

    def finish(d):
        found = chip_sum(d, place)
        for i in range(1, line):
            there = along(i)
            line_copy(d, i, there, there).wait_recv()
            found = found + line_in[d, there].astype(jnp.float32)
        for h in range(own):
            grad_ref[d, :, h * LANES : (h + 1) * LANES] = found[h] * (1.0 / norm_scale)

    exposure_part[...] = jnp.zeros_like(exposure_part)
    quarter = blocks // 4
    for i in range(1, line):
        forward(0, (i - 1) * quarter, i * quarter)
        line_step(1, i)
    forward(0, (line - 1) * quarter, blocks)
    exposure_send(0)
    for i in range(line):
        row_step(1, i)
    core_steps(1)
    forward(1, 0, blocks // 2)
    exposure_sum(0)
    forward(1, blocks // 2, blocks)
    exposure_send(1)
    grad = exposure_grad(0)
    backward(0, grad, 0, blocks // 2)
    exposure_sum(1)
    backward(0, grad, blocks // 2, blocks)
    add_up()
    core_stage(0)
    grad = exposure_grad(1)
    backward(1, grad, 0, blocks // 2)
    row_stage(0)
    backward(1, grad, blocks // 2, blocks)
    add_up()
    core_stage(1)
    line_stage(0)
    row_stage(1)
    line_stage(1)
    for d in range(dates):
        finish(d)

    for d in range(dates):
        for k in range(1, 4 * line):
            panel_copy(d, me, core_peer, k).wait_send()
        others(lambda t: piece_copy(d, t, me).wait_send())
        others(lambda t: full_copy(d, t, me).wait_send())
        for z in range(line):
            for y in range(ROWS):
                core_copy(d, y, z).wait_send()
            row_copy(d, z).wait_send()
        for i in range(1, line):
            line_copy(d, i, place, along(i)).wait_send()


def per_device_fused(
    panels,
    lin_weight,
    quad_weight,
    positions,
    pattern,
    netting,
    default_curve,
    date_ids,
    loss_given,
):
    size = lax.axis_size("trade")
    line = size // (CORES * ROWS)
    blocks, width = positions.shape
    dates, scen, columns = panels.shape
    own = columns // width
    fblocks = own * size
    terms = blocks * PICKS
    norm_scale = (NETS / (blocks * width * size)) ** 0.5
    flat = pattern.reshape(-1)
    at = jnp.arange(terms, dtype=jnp.int32)
    ahead = (flat[None, :] < flat[:, None]) | (
        (flat[None, :] == flat[:, None]) & (at[None, :] < at[:, None])
    )
    rank = jnp.sum(ahead, axis=1, dtype=jnp.int32)
    order = jnp.sum(jnp.where(rank[None, :] == at[:, None], at[None, :], 0), axis=1)
    ids = jnp.arange(fblocks, dtype=jnp.int32)
    first = jnp.sum(flat[None, :] < ids[:, None], axis=1, dtype=jnp.int32)
    count = jnp.sum(flat[None, :] == ids[:, None], axis=1, dtype=jnp.int32)
    last = jnp.maximum(first + count - 1, 0)
    used = (count > 0).astype(jnp.float32)
    keep = 1.0 - jnp.any(first[None, :] == at[:, None], axis=1).astype(jnp.float32)

    smem = pl.BlockSpec(memory_space=pltpu.SMEM)
    vmem = pl.BlockSpec(memory_space=pltpu.VMEM)
    hbm = pl.BlockSpec(memory_space=pl.ANY)
    tile = (scen, width)
    f32, bf16 = jnp.float32, jnp.bfloat16
    dma = pltpu.SemaphoreType.DMA
    charge, panel_grad = pl.pallas_call(
        functools.partial(fused_kernel, size, line, norm_scale),
        out_shape=(
            jax.ShapeDtypeStruct((dates,), f32),
            jax.ShapeDtypeStruct((dates, scen, columns), f32),
        ),
        in_specs=[smem] * 8 + [vmem] * 3 + [hbm] * 2,
        out_specs=(smem, vmem),
        scratch_shapes=[
            pltpu.VMEM((blocks, PICKS * width, width), bf16),
            pltpu.VMEM((blocks, PICKS * width, width), bf16),
            pltpu.VMEM((fblocks,) + tile, bf16),
            pltpu.VMEM((fblocks,) + tile, bf16),
            pltpu.VMEM((dates, blocks) + tile, f32),
            pltpu.VMEM((dates, blocks) + tile, f32),
            pltpu.VMEM((dates, scen, NETS), f32),
            pltpu.VMEM((dates, size, scen // size, NETS), f32),
            pltpu.VMEM((dates, scen, NETS), f32),
            pltpu.VMEM((terms,) + tile, f32),
            pltpu.VMEM((terms,) + tile, f32),
            pltpu.VMEM((dates, ROWS * line, own) + tile, bf16),
            pltpu.VMEM((dates, ROWS * line, own) + tile, bf16),
            pltpu.VMEM((dates, ROWS * line, own) + tile, f32),
            pltpu.VMEM((dates, line, own) + tile, bf16),
            pltpu.VMEM((dates, line, own) + tile, bf16),
            pltpu.VMEM((dates, line, own) + tile, bf16),
            pltpu.VMEM((dates, line, own) + tile, bf16),
            dma((2,)),
            dma((dates, 4 * line)),
            dma((dates, size)),
            dma((dates, size)),
            dma((dates, size)),
            dma((dates, size)),
            dma((dates, size)),
            dma((dates, ROWS * line)),
            dma((dates, ROWS * line)),
            dma((dates, line)),
            dma((dates, line)),
            dma((dates, line)),
            dma((dates, line)),
        ],
        compiler_params=pltpu.CompilerParams(
            collective_id=0, has_side_effects=True, vmem_limit_bytes=56 * 1024 * 1024
        ),
        name="fused",
    )(
        order, last, flat, netting, date_ids, default_curve, keep, used,
        panels, positions, loss_given.reshape(1, -1),
        lin_weight.reshape(blocks, PICKS * width, width),
        quad_weight.reshape(blocks, PICKS * width, width),
    )
    return (charge, panel_grad)


def fits_kernel(mesh, panels, positions, loss_given):
    size = mesh.shape["trade"]
    width = positions.shape[1]
    line = size // (CORES * ROWS)
    return (
        panels.shape[0] == 2
        and width == LANES
        and line * CORES * ROWS == size
        and line == 4
        and (panels.shape[2] // size) % width == 0
        and (panels.shape[1] // mesh.shape["parts"]) % (8 * size) == 0
    )


def solution(mesh):
    in_specs = (
        P(None, "parts", "trade"),
        P(("parts", "trade"), None, None, None),
        P(("parts", "trade"), None, None, None),
        P(("parts", "trade"), None),
        P(("parts", "trade"), None),
        P(("parts", "trade")),
        P(),
        P(),
        P("parts"),
    )
    out_specs = (P("parts"), P(None, "parts", "trade"))

    def run(*args):
        body = per_device_fused if fits_kernel(mesh, args[0], args[3], args[8]) else per_device
        return jax.shard_map(
            body, mesh=mesh, in_specs=in_specs, out_specs=out_specs, check_vma=False
        )(*args)

    return run
```

```python
import functools

import jax
import jax.numpy as jnp
from jax import lax
from jax.experimental import pallas as pl
from jax.experimental.pallas import tpu as pltpu
from jax.sharding import PartitionSpec as P

PICKS = 4
NETS = 128


def per_device(
    panels,
    lin_weight,
    quad_weight,
    positions,
    pattern,
    netting,
    default_curve,
    date_ids,
    loss_given,
):
    devices = lax.axis_size("trade")
    local_blocks, block_width = positions.shape
    trades_all = local_blocks * block_width * devices
    norm_scale = (NETS / trades_all) ** 0.5
    grad_unit = 1.0 / norm_scale
    factors = panels.shape[2] * devices
    fblocks = factors // block_width
    horizon = jnp.arange(default_curve.shape[0], dtype=jnp.int32)
    weights = jnp.sum(
        jnp.where(date_ids[:, None] == horizon[None, :], default_curve[None, :], 0.0), axis=1
    )
    set_map = (netting[:, None] == jnp.arange(NETS, dtype=jnp.int32)[None, :]).astype(jnp.float32)
    flat_pattern = pattern.reshape(-1)
    block_map = (flat_pattern[:, None] == jnp.arange(fblocks, dtype=jnp.int32)[None, :]).astype(
        jnp.float32
    )
    gathered = lax.all_gather(panels, "trade", axis=2, tiled=True)
    leading = gathered.shape[:-1]
    blocks = gathered.reshape(leading + (fblocks, block_width))
    picked = jnp.take(blocks, flat_pattern, axis=-2).reshape(
        leading + (local_blocks, PICKS, block_width)
    )
    linear = jnp.einsum(
        "...bkc,bkct->...bt", picked, lin_weight, preferred_element_type=jnp.float32
    )
    square_term = jnp.einsum(
        "...bkc,bkct->...bt", picked, quad_weight, preferred_element_type=jnp.float32
    )
    trade_state = linear + 0.25 * square_term * square_term
    block_sum = jnp.sum(positions * jax.nn.softplus(trade_state), axis=-1)
    local_exposure = norm_scale * jnp.einsum(
        "...b,bn->...n", block_sum, set_map, precision=lax.Precision.HIGHEST
    )
    local_exposure, square_term, trade_state = (local_exposure, square_term, trade_state)
    exposure = lax.psum(local_exposure, "trade")
    losses = jnp.sum(loss_given * jax.nn.softplus(exposure), axis=-1)
    charge = weights * jnp.mean(losses, axis=-1)
    exposure_grad = weights[:, None, None] * loss_given * jax.nn.sigmoid(exposure)
    block_adjoint = norm_scale * jnp.einsum(
        "...n,bn->...b", exposure_grad, set_map, precision=lax.Precision.HIGHEST
    )
    state_adjoint = block_adjoint[..., None] * positions * jax.nn.sigmoid(trade_state)
    adjoint_lin = state_adjoint.astype(jnp.bfloat16)
    adjoint_square = (0.5 * square_term * state_adjoint).astype(jnp.bfloat16)
    contrib = jnp.einsum(
        "...bt,bkct->...bkc", adjoint_lin, lin_weight, preferred_element_type=jnp.float32
    )
    contrib = contrib + jnp.einsum(
        "...bt,bkct->...bkc", adjoint_square, quad_weight, preferred_element_type=jnp.float32
    )
    leading = contrib.shape[:-3]
    flat_contrib = contrib.reshape(leading + (local_blocks * PICKS, block_width))
    leading = flat_contrib.shape[:-2]
    placed = jnp.einsum("...jc,jf->...fc", flat_contrib, block_map, precision=lax.Precision.HIGHEST)
    panel_grad = lax.psum_scatter(
        (grad_unit * placed).reshape(leading + (factors,)), "trade", scatter_dimension=2, tiled=True
    )
    return (charge, panel_grad)


MESH = pl.DeviceIdType.MESH
LANES = 128
CORES = 2
ROWS = 2
UNROLL = 8
TRANSPOSED = (((1,), (1,)), ((), ()))


def fused_kernel(
    size,
    line,
    norm_scale,
    order_ref,
    last_ref,
    pattern_ref,
    netting_ref,
    dates_ref,
    curve_ref,
    keep_ref,
    used_ref,
    panels_ref,
    positions_ref,
    loss_ref,
    lin_hbm,
    quad_hbm,
    charge_ref,
    grad_ref,
    lin,
    quad,
    panels_a,
    panels_b,
    slope,
    half_square,
    exposure_part,
    exposure_pieces,
    exposure_full,
    contrib,
    running,
    core_out,
    core_in,
    kept,
    row_out,
    row_in,
    line_out,
    line_in,
    weight_sem,
    gather_send,
    gather_recv,
    piece_send,
    piece_recv,
    full_send,
    full_recv,
    core_send,
    core_recv,
    row_send,
    row_recv,
    line_send,
    line_recv,
):
    me = lax.axis_index("trade")
    core = lax.rem(me, CORES)
    row = lax.rem(me // CORES, ROWS)
    place = me // (CORES * ROWS)
    blocks = positions_ref.shape[0]
    scen = panels_ref.shape[1]
    own = panels_ref.shape[2] // LANES
    piece = scen // size
    gathered = (panels_a, panels_b)
    dates = len(gathered)

    def index(z, y, c):
        return (z * ROWS + y) * CORES + c

    def along(i):
        return lax.rem(place + i, line)

    def copy(src, dst, send, recv, peer):
        return pltpu.make_async_remote_copy(
            src_ref=src, dst_ref=dst, send_sem=send, recv_sem=recv,
            device_id={"trade": peer}, device_id_type=MESH,
        )

    row_peer = index(place, 1 - row, core)
    core_peer = index(place, row, 1 - core)

    weight_copies = [
        pltpu.make_async_copy(lin_hbm, lin, weight_sem.at[0]),
        pltpu.make_async_copy(quad_hbm, quad, weight_sem.at[1]),
    ]
    for each in weight_copies:
        each.start()

    for d in range(dates):
        for h in range(own):
            gathered[d][me * own + h] = panels_ref[d, :, h * LANES : (h + 1) * LANES]

    barrier = pltpu.get_barrier_semaphore()

    @pl.loop(1, size)
    def _(i):
        pl.semaphore_signal(
            barrier, inc=1, device_id={"trade": lax.rem(me + i, size)}, device_id_type=MESH
        )

    pl.semaphore_wait(barrier, size - 1)

    def panel_copy(d, slot, peer, k):
        part = gathered[d].at[pl.ds(slot * own, own)]
        return copy(part, part, gather_send.at[d, k], gather_recv.at[d, slot], peer)

    def to_right(d, z):
        return panel_copy(d, index(z, row, core), index(place + 1, row, core), z)

    def to_left(d, z):
        return panel_copy(d, index(z, row, core), index(place - 1, row, core), line + z)

    def to_row(d, z):
        return panel_copy(d, index(z, row, core), row_peer, 2 * line + z)

    def to_core(d, z, y, k):
        return panel_copy(d, index(z, y, core), core_peer, k + z)

    def panel_wait(d, slot):
        panel_copy(d, slot, core_peer, 0).wait_recv()

    def goes_right(z):
        return jnp.logical_and(z <= place, place < line - 1)

    def goes_left(z):
        return jnp.logical_and(z >= place, place > 0)

    def pass_on(d, z):
        @pl.when(goes_right(z))
        def _():
            to_right(d, z).start()

        @pl.when(goes_left(z))
        def _():
            to_left(d, z).start()

        to_row(d, z).start()
        to_core(d, z, row, 3 * line).start()

    def both_sides(s, act):
        @pl.when(place >= s)
        def _():
            act(place - s)

        if s > 0:
            @pl.when(place + s < line)
            def _():
                act(place + s)

    def line_step(d, s):
        def act(z):
            panel_wait(d, index(z, row, core))
            pass_on(d, z)

        both_sides(s, act)

    def row_step(d, s):
        def act(z):
            panel_wait(d, index(z, 1 - row, core))
            to_core(d, z, 1 - row, 4 * line).start()

        both_sides(s, act)

    def core_steps(d):
        for z in range(line):
            for y in range(ROWS):
                panel_wait(d, index(z, y, 1 - core))

    pass_on(0, place)
    line_step(0, 1)
    pass_on(1, place)
    row_step(0, 0)
    for s in range(2, line):
        line_step(0, s)
        row_step(0, s - 1)
    row_step(0, line - 1)
    core_steps(0)
    for each in weight_copies:
        each.wait()

    lane = lax.broadcasted_iota(jnp.int32, (1, LANES), 1)

    def forward(d, first, stop):
        @pl.loop(first, stop, unroll=UNROLL)
        def _(b):
            picked = jnp.concatenate(
                [gathered[d][pattern_ref[b * PICKS + k]] for k in range(PICKS)], axis=1
            )
            both = jnp.concatenate([lin[b], quad[b]], axis=1)
            terms = jnp.dot(picked, both, preferred_element_type=jnp.float32)
            square = terms[:, LANES:]
            state = terms[:, :LANES] + 0.25 * square * square
            small = jnp.exp(-jnp.abs(state))
            above = 1.0 + small
            soft = jnp.maximum(state, 0.0) + jnp.log(above)
            sigmoid = jnp.where(state >= 0.0, 1.0, small) / above
            held = positions_ref[pl.ds(b, 1), :]
            block_sum = jnp.sum(held * soft, axis=1, keepdims=True)
            in_set = jnp.where(lane == netting_ref[b], norm_scale, 0.0)
            exposure_part[d] += block_sum * in_set
            slope[d, b] = held * sigmoid
            half_square[d, b] = 0.5 * square

    def piece_rows(t):
        return pl.ds(pl.multiple_of(t * piece, piece), piece)

    def piece_copy(d, t, source):
        return copy(
            exposure_part.at[d, piece_rows(t)], exposure_pieces.at[d, source],
            piece_send.at[d, t], piece_recv.at[d, source], t,
        )

    def full_copy(d, t, source):
        return copy(
            exposure_full.at[d, piece_rows(source)], exposure_full.at[d, piece_rows(source)],
            full_send.at[d, t], full_recv.at[d, source], t,
        )

    def others(act):
        @pl.loop(1, size)
        def _(i):
            act(lax.rem(me + i, size))

    def exposure_send(d):
        exposure_pieces[d, me] = exposure_part[d, piece_rows(me), :]
        others(lambda t: piece_copy(d, t, me).start())

    def exposure_sum(d):
        others(lambda t: piece_copy(d, t, t).wait_recv())
        exposure_full[d, piece_rows(me), :] = jnp.sum(exposure_pieces[d], axis=0)
        others(lambda t: full_copy(d, t, me).start())

    def exposure_grad(d):
        others(lambda t: full_copy(d, t, t).wait_recv())
        exposure = exposure_full[d]
        small = jnp.exp(-jnp.abs(exposure))
        above = 1.0 + small
        loss = loss_ref[...]
        weight = curve_ref[dates_ref[d]]
        soft = jnp.maximum(exposure, 0.0) + jnp.log(above)
        charge_ref[d] = weight * (jnp.sum(loss * soft) * (1.0 / scen))
        return weight * loss * (jnp.where(exposure >= 0.0, 1.0, small) / above)

    def backward(d, grad, first, stop):
        @pl.loop(first, stop, unroll=UNROLL)
        def _(b):
            in_set = jnp.where(lane == netting_ref[b], norm_scale, 0.0)
            adjoint = jnp.sum(grad * in_set, axis=1, keepdims=True) * slope[d, b]
            sent = jnp.concatenate(
                [
                    adjoint.astype(jnp.bfloat16),
                    (half_square[d, b] * adjoint).astype(jnp.bfloat16),
                ],
                axis=1,
            )
            both = jnp.concatenate([lin[b], quad[b]], axis=1)
            out = lax.dot_general(sent, both, TRANSPOSED, preferred_element_type=jnp.float32)
            for k in range(PICKS):
                contrib[b * PICKS + k] = out[:, k * LANES : (k + 1) * LANES]

    def add_up():
        running[0] = contrib[order_ref[0]]

        @pl.loop(1, blocks * PICKS, unroll=UNROLL)
        def _(j):
            running[j] = contrib[order_ref[j]] + keep_ref[j] * running[j - 1]

    def total(slot, h):
        p = slot * own + h
        return running[last_ref[p]] * used_ref[p]

    def core_copy(d, y, z):
        at = d, y * line + z
        return copy(core_out.at[at], core_in.at[at], core_send.at[at], core_recv.at[at], core_peer)

    def row_copy(d, z):
        at = d, z
        return copy(row_out.at[at], row_in.at[at], row_send.at[at], row_recv.at[at], row_peer)

    def line_copy(d, i, here, there):
        return copy(
            line_out.at[d, i], line_in.at[d, here], line_send.at[d, i], line_recv.at[d, here],
            index(there, row, core),
        )

    def core_stage(d):
        for y in (1 - row, row):
            @pl.loop(0, line)
            def _(z):
                for h in range(own):
                    core_out[d, y * line + z, h] = total(index(z, y, 1 - core), h).astype(
                        jnp.bfloat16
                    )
                core_copy(d, y, z).start()

        for y in (1 - row, row):
            @pl.loop(0, line)
            def _(z):
                for h in range(own):
                    kept[d, y * line + z, h] = total(index(z, y, core), h)

    def row_stage(d):
        @pl.loop(0, line)
        def _(z):
            core_copy(d, 1 - row, z).wait_recv()
            at = (1 - row) * line + z
            row_out[d, z] = (kept[d, at] + core_in[d, at].astype(jnp.float32)).astype(jnp.bfloat16)
            row_copy(d, z).start()

    def chip_sum(d, z):
        core_copy(d, row, z).wait_recv()
        row_copy(d, z).wait_recv()
        at = row * line + z
        return (
            kept[d, at]
            + core_in[d, at].astype(jnp.float32)
            + row_in[d, z].astype(jnp.float32)
        )

    def line_stage(d):
        for i in range(1, line):
            there = along(i)
            line_out[d, i] = chip_sum(d, there).astype(jnp.bfloat16)
            line_copy(d, i, place, there).start()

    def finish(d):
        found = chip_sum(d, place)
        for i in range(1, line):
            there = along(i)
            line_copy(d, i, there, there).wait_recv()
            found = found + line_in[d, there].astype(jnp.float32)
        for h in range(own):
            grad_ref[d, :, h * LANES : (h + 1) * LANES] = found[h] * (1.0 / norm_scale)

    exposure_part[...] = jnp.zeros_like(exposure_part)
    share = blocks // line
    for s in range(1, line):
        forward(0, (s - 1) * share, s * share)
        line_step(1, s)
        row_step(1, s - 1)
    forward(0, (line - 1) * share, blocks)
    exposure_send(0)
    row_step(1, line - 1)
    core_steps(1)
    exposure_sum(0)
    forward(1, 0, blocks)
    exposure_send(1)
    grad = exposure_grad(0)
    backward(0, grad, 0, blocks // 2)
    exposure_sum(1)
    backward(0, grad, blocks // 2, blocks)
    add_up()
    core_stage(0)
    grad = exposure_grad(1)
    backward(1, grad, 0, blocks // 2)
    row_stage(0)
    backward(1, grad, blocks // 2, blocks)
    add_up()
    core_stage(1)
    row_stage(1)
    for d in range(dates):
        line_stage(d)
    for d in range(dates):
        finish(d)

    for d in range(dates):
        for z in range(line):
            @pl.when(goes_right(z))
            def _():
                to_right(d, z).wait_send()

            @pl.when(goes_left(z))
            def _():
                to_left(d, z).wait_send()

            to_row(d, z).wait_send()
            to_core(d, z, row, 3 * line).wait_send()
            to_core(d, z, 1 - row, 4 * line).wait_send()
        others(lambda t: piece_copy(d, t, me).wait_send())
        others(lambda t: full_copy(d, t, me).wait_send())
        for z in range(line):
            for y in range(ROWS):
                core_copy(d, y, z).wait_send()
            row_copy(d, z).wait_send()
        for i in range(1, line):
            line_copy(d, i, place, along(i)).wait_send()


def per_device_fused(
    panels,
    lin_weight,
    quad_weight,
    positions,
    pattern,
    netting,
    default_curve,
    date_ids,
    loss_given,
):
    size = lax.axis_size("trade")
    line = size // (CORES * ROWS)
    blocks, width = positions.shape
    dates, scen, columns = panels.shape
    own = columns // width
    fblocks = own * size
    terms = blocks * PICKS
    norm_scale = (NETS / (blocks * width * size)) ** 0.5
    flat = pattern.reshape(-1)
    at = jnp.arange(terms, dtype=jnp.int32)
    ahead = (flat[None, :] < flat[:, None]) | (
        (flat[None, :] == flat[:, None]) & (at[None, :] < at[:, None])
    )
    rank = jnp.sum(ahead, axis=1, dtype=jnp.int32)
    order = jnp.sum(jnp.where(rank[None, :] == at[:, None], at[None, :], 0), axis=1)
    ids = jnp.arange(fblocks, dtype=jnp.int32)
    first = jnp.sum(flat[None, :] < ids[:, None], axis=1, dtype=jnp.int32)
    count = jnp.sum(flat[None, :] == ids[:, None], axis=1, dtype=jnp.int32)
    last = jnp.maximum(first + count - 1, 0)
    used = (count > 0).astype(jnp.float32)
    keep = 1.0 - jnp.any(first[None, :] == at[:, None], axis=1).astype(jnp.float32)

    smem = pl.BlockSpec(memory_space=pltpu.SMEM)
    vmem = pl.BlockSpec(memory_space=pltpu.VMEM)
    hbm = pl.BlockSpec(memory_space=pl.ANY)
    tile = (scen, width)
    f32, bf16 = jnp.float32, jnp.bfloat16
    dma = pltpu.SemaphoreType.DMA
    charge, panel_grad = pl.pallas_call(
        functools.partial(fused_kernel, size, line, norm_scale),
        out_shape=(
            jax.ShapeDtypeStruct((dates,), f32),
            jax.ShapeDtypeStruct((dates, scen, columns), f32),
        ),
        in_specs=[smem] * 8 + [vmem] * 3 + [hbm] * 2,
        out_specs=(smem, vmem),
        scratch_shapes=[
            pltpu.VMEM((blocks, PICKS * width, width), bf16),
            pltpu.VMEM((blocks, PICKS * width, width), bf16),
            pltpu.VMEM((fblocks,) + tile, bf16),
            pltpu.VMEM((fblocks,) + tile, bf16),
            pltpu.VMEM((dates, blocks) + tile, f32),
            pltpu.VMEM((dates, blocks) + tile, f32),
            pltpu.VMEM((dates, scen, NETS), f32),
            pltpu.VMEM((dates, size, scen // size, NETS), f32),
            pltpu.VMEM((dates, scen, NETS), f32),
            pltpu.VMEM((terms,) + tile, f32),
            pltpu.VMEM((terms,) + tile, f32),
            pltpu.VMEM((dates, ROWS * line, own) + tile, bf16),
            pltpu.VMEM((dates, ROWS * line, own) + tile, bf16),
            pltpu.VMEM((dates, ROWS * line, own) + tile, f32),
            pltpu.VMEM((dates, line, own) + tile, bf16),
            pltpu.VMEM((dates, line, own) + tile, bf16),
            pltpu.VMEM((dates, line, own) + tile, bf16),
            pltpu.VMEM((dates, line, own) + tile, bf16),
            dma((2,)),
            dma((dates, 5 * line)),
            dma((dates, size)),
            dma((dates, size)),
            dma((dates, size)),
            dma((dates, size)),
            dma((dates, size)),
            dma((dates, ROWS * line)),
            dma((dates, ROWS * line)),
            dma((dates, line)),
            dma((dates, line)),
            dma((dates, line)),
            dma((dates, line)),
        ],
        compiler_params=pltpu.CompilerParams(
            collective_id=0, has_side_effects=True, vmem_limit_bytes=56 * 1024 * 1024
        ),
        name="fused",
    )(
        order, last, flat, netting, date_ids, default_curve, keep, used,
        panels, positions, loss_given.reshape(1, -1),
        lin_weight.reshape(blocks, PICKS * width, width),
        quad_weight.reshape(blocks, PICKS * width, width),
    )
    return (charge, panel_grad)


def fits_kernel(mesh, panels, positions, loss_given):
    size = mesh.shape["trade"]
    width = positions.shape[1]
    line = size // (CORES * ROWS)
    return (
        panels.shape[0] == 2
        and width == LANES
        and line * CORES * ROWS == size
        and line == 4
        and (panels.shape[2] // size) % width == 0
        and (panels.shape[1] // mesh.shape["parts"]) % (8 * size) == 0
    )


def solution(mesh):
    in_specs = (
        P(None, "parts", "trade"),
        P(("parts", "trade"), None, None, None),
        P(("parts", "trade"), None, None, None),
        P(("parts", "trade"), None),
        P(("parts", "trade"), None),
        P(("parts", "trade")),
        P(),
        P(),
        P("parts"),
    )
    out_specs = (P("parts"), P(None, "parts", "trade"))

    def run(*args):
        body = per_device_fused if fits_kernel(mesh, args[0], args[3], args[8]) else per_device
        return jax.shard_map(
            body, mesh=mesh, in_specs=in_specs, out_specs=out_specs, check_vma=False
        )(*args)

    return run
```

```python
import functools

import jax
import jax.numpy as jnp
from jax import lax
from jax.experimental import pallas as pl
from jax.experimental.pallas import tpu as pltpu
from jax.sharding import PartitionSpec as P

PICKS = 4
NETS = 128


def per_device(
    panels,
    lin_weight,
    quad_weight,
    positions,
    pattern,
    netting,
    default_curve,
    date_ids,
    loss_given,
):
    devices = lax.axis_size("trade")
    local_blocks, block_width = positions.shape
    trades_all = local_blocks * block_width * devices
    norm_scale = (NETS / trades_all) ** 0.5
    grad_unit = 1.0 / norm_scale
    factors = panels.shape[2] * devices
    fblocks = factors // block_width
    horizon = jnp.arange(default_curve.shape[0], dtype=jnp.int32)
    weights = jnp.sum(
        jnp.where(date_ids[:, None] == horizon[None, :], default_curve[None, :], 0.0), axis=1
    )
    set_map = (netting[:, None] == jnp.arange(NETS, dtype=jnp.int32)[None, :]).astype(jnp.float32)
    flat_pattern = pattern.reshape(-1)
    block_map = (flat_pattern[:, None] == jnp.arange(fblocks, dtype=jnp.int32)[None, :]).astype(
        jnp.float32
    )
    gathered = lax.all_gather(panels, "trade", axis=2, tiled=True)
    leading = gathered.shape[:-1]
    blocks = gathered.reshape(leading + (fblocks, block_width))
    picked = jnp.take(blocks, flat_pattern, axis=-2).reshape(
        leading + (local_blocks, PICKS, block_width)
    )
    linear = jnp.einsum(
        "...bkc,bkct->...bt", picked, lin_weight, preferred_element_type=jnp.float32
    )
    square_term = jnp.einsum(
        "...bkc,bkct->...bt", picked, quad_weight, preferred_element_type=jnp.float32
    )
    trade_state = linear + 0.25 * square_term * square_term
    block_sum = jnp.sum(positions * jax.nn.softplus(trade_state), axis=-1)
    local_exposure = norm_scale * jnp.einsum(
        "...b,bn->...n", block_sum, set_map, precision=lax.Precision.HIGHEST
    )
    local_exposure, square_term, trade_state = (local_exposure, square_term, trade_state)
    exposure = lax.psum(local_exposure, "trade")
    losses = jnp.sum(loss_given * jax.nn.softplus(exposure), axis=-1)
    charge = weights * jnp.mean(losses, axis=-1)
    exposure_grad = weights[:, None, None] * loss_given * jax.nn.sigmoid(exposure)
    block_adjoint = norm_scale * jnp.einsum(
        "...n,bn->...b", exposure_grad, set_map, precision=lax.Precision.HIGHEST
    )
    state_adjoint = block_adjoint[..., None] * positions * jax.nn.sigmoid(trade_state)
    adjoint_lin = state_adjoint.astype(jnp.bfloat16)
    adjoint_square = (0.5 * square_term * state_adjoint).astype(jnp.bfloat16)
    contrib = jnp.einsum(
        "...bt,bkct->...bkc", adjoint_lin, lin_weight, preferred_element_type=jnp.float32
    )
    contrib = contrib + jnp.einsum(
        "...bt,bkct->...bkc", adjoint_square, quad_weight, preferred_element_type=jnp.float32
    )
    leading = contrib.shape[:-3]
    flat_contrib = contrib.reshape(leading + (local_blocks * PICKS, block_width))
    leading = flat_contrib.shape[:-2]
    placed = jnp.einsum("...jc,jf->...fc", flat_contrib, block_map, precision=lax.Precision.HIGHEST)
    panel_grad = lax.psum_scatter(
        (grad_unit * placed).reshape(leading + (factors,)), "trade", scatter_dimension=2, tiled=True
    )
    return (charge, panel_grad)


MESH = pl.DeviceIdType.MESH
LANES = 128
CORES = 2
ROWS = 2
UNROLL = 8
TRANSPOSED = (((1,), (1,)), ((), ()))


def fused_kernel(
    size,
    line,
    norm_scale,
    plan_ref,
    pattern_ref,
    netting_ref,
    dates_ref,
    curve_ref,
    panels_ref,
    positions_ref,
    loss_ref,
    lin_hbm,
    quad_hbm,
    charge_ref,
    grad_ref,
    lin,
    quad,
    panels_a,
    panels_b,
    slope,
    half_square,
    exposure_part,
    exposure_pieces,
    exposure_full,
    contrib,
    running,
    core_out,
    core_in,
    kept,
    row_out,
    row_in,
    line_out,
    line_in,
    weight_sem,
    gather_send,
    gather_recv,
    piece_send,
    piece_recv,
    full_send,
    full_recv,
    core_send,
    core_recv,
    row_send,
    row_recv,
    line_send,
    line_recv,
):
    me = lax.axis_index("trade")
    core = lax.rem(me, CORES)
    row = lax.rem(me // CORES, ROWS)
    place = me // (CORES * ROWS)
    blocks = positions_ref.shape[0]
    scen = panels_ref.shape[1]
    own = panels_ref.shape[2] // LANES
    piece = scen // size
    terms = blocks * PICKS
    fblocks = own * size
    gathered = (panels_a, panels_b)
    dates = len(gathered)

    def index(z, y, c):
        return (z * ROWS + y) * CORES + c

    def along(i):
        return lax.rem(place + i, line)

    def copy(src, dst, send, recv, peer):
        return pltpu.make_async_remote_copy(
            src_ref=src, dst_ref=dst, send_sem=send, recv_sem=recv,
            device_id={"trade": peer}, device_id_type=MESH,
        )

    row_peer = index(place, 1 - row, core)
    core_peer = index(place, row, 1 - core)

    weight_copies = [
        pltpu.make_async_copy(lin_hbm, lin, weight_sem.at[0]),
        pltpu.make_async_copy(quad_hbm, quad, weight_sem.at[1]),
    ]
    for each in weight_copies:
        each.start()

    for d in range(dates):
        for h in range(own):
            gathered[d][me * own + h] = panels_ref[d, :, h * LANES : (h + 1) * LANES]

    barrier = pltpu.get_barrier_semaphore()

    @pl.loop(1, size)
    def _(i):
        pl.semaphore_signal(
            barrier, inc=1, device_id={"trade": lax.rem(me + i, size)}, device_id_type=MESH
        )

    pl.semaphore_wait(barrier, size - 1)

    def panel_copy(d, slot, peer, k):
        part = gathered[d].at[pl.ds(slot * own, own)]
        return copy(part, part, gather_send.at[d, k], gather_recv.at[d, slot], peer)

    def to_right(d, z):
        return panel_copy(d, index(z, row, core), index(place + 1, row, core), z)

    def to_left(d, z):
        return panel_copy(d, index(z, row, core), index(place - 1, row, core), line + z)

    def to_row(d, z):
        return panel_copy(d, index(z, row, core), row_peer, 2 * line + z)

    def to_core(d, z, y, k):
        return panel_copy(d, index(z, y, core), core_peer, k + z)

    def panel_wait(d, slot):
        panel_copy(d, slot, core_peer, 0).wait_recv()

    def goes_right(z):
        return jnp.logical_and(z <= place, place < line - 1)

    def goes_left(z):
        return jnp.logical_and(z >= place, place > 0)

    def pass_on(d, z):
        @pl.when(goes_right(z))
        def _():
            to_right(d, z).start()

        @pl.when(goes_left(z))
        def _():
            to_left(d, z).start()

        to_row(d, z).start()
        to_core(d, z, row, 3 * line).start()

    def both_sides(s, act):
        @pl.when(place >= s)
        def _():
            act(place - s)

        if s > 0:
            @pl.when(place + s < line)
            def _():
                act(place + s)

    def line_step(d, s):
        def act(z):
            panel_wait(d, index(z, row, core))
            pass_on(d, z)

        both_sides(s, act)

    def row_step(d, s):
        def act(z):
            panel_wait(d, index(z, 1 - row, core))
            to_core(d, z, 1 - row, 4 * line).start()

        both_sides(s, act)

    def core_steps(d):
        for z in range(line):
            for y in range(ROWS):
                panel_wait(d, index(z, y, 1 - core))

    pass_on(0, place)
    pass_on(1, place)
    line_step(0, 1)
    row_step(0, 0)
    for s in range(2, line):
        line_step(1, s - 1)
        line_step(0, s)
        row_step(1, s - 2)
        row_step(0, s - 1)
    line_step(1, line - 1)
    row_step(0, line - 1)
    core_steps(0)
    for each in weight_copies:
        each.wait()

    lane = lax.broadcasted_iota(jnp.int32, (1, LANES), 1)

    def forward(d, first, stop):
        @pl.loop(first, stop, unroll=UNROLL)
        def _(b):
            picked = jnp.concatenate(
                [gathered[d][pattern_ref[b * PICKS + k]] for k in range(PICKS)], axis=1
            )
            both = jnp.concatenate([lin[b], quad[b]], axis=1)
            terms = jnp.dot(picked, both, preferred_element_type=jnp.float32)
            square = terms[:, LANES:]
            state = terms[:, :LANES] + 0.25 * square * square
            small = jnp.exp(-jnp.abs(state))
            above = 1.0 + small
            soft = jnp.maximum(state, 0.0) + jnp.log(above)
            sigmoid = jnp.where(state >= 0.0, 1.0, small) / above
            held = positions_ref[pl.ds(b, 1), :]
            block_sum = jnp.sum(held * soft, axis=1, keepdims=True)
            in_set = jnp.where(lane == netting_ref[b], norm_scale, 0.0)
            exposure_part[d] += block_sum * in_set
            slope[d, b] = held * sigmoid
            half_square[d, b] = 0.5 * square

    def piece_rows(t):
        return pl.ds(pl.multiple_of(t * piece, piece), piece)

    def piece_copy(d, t, source):
        return copy(
            exposure_part.at[d, piece_rows(t)], exposure_pieces.at[d, source],
            piece_send.at[d, t], piece_recv.at[d, source], t,
        )

    def full_copy(d, t, source):
        return copy(
            exposure_full.at[d, piece_rows(source)], exposure_full.at[d, piece_rows(source)],
            full_send.at[d, t], full_recv.at[d, source], t,
        )

    def others(act):
        @pl.loop(1, size)
        def _(i):
            act(lax.rem(me + i, size))

    def exposure_send(d):
        exposure_pieces[d, me] = exposure_part[d, piece_rows(me), :]
        others(lambda t: piece_copy(d, t, me).start())

    def exposure_sum(d):
        others(lambda t: piece_copy(d, t, t).wait_recv())
        exposure_full[d, piece_rows(me), :] = jnp.sum(exposure_pieces[d], axis=0)
        others(lambda t: full_copy(d, t, me).start())

    def exposure_grad(d):
        others(lambda t: full_copy(d, t, t).wait_recv())
        exposure = exposure_full[d]
        small = jnp.exp(-jnp.abs(exposure))
        above = 1.0 + small
        loss = loss_ref[...]
        weight = curve_ref[dates_ref[d]]
        soft = jnp.maximum(exposure, 0.0) + jnp.log(above)
        charge_ref[d] = weight * (jnp.sum(loss * soft) * (1.0 / scen))
        return weight * loss * (jnp.where(exposure >= 0.0, 1.0, small) / above)

    def backward(d, grad, first, stop):
        @pl.loop(first, stop, unroll=UNROLL)
        def _(b):
            in_set = jnp.where(lane == netting_ref[b], norm_scale, 0.0)
            adjoint = jnp.sum(grad * in_set, axis=1, keepdims=True) * slope[d, b]
            sent = jnp.concatenate(
                [
                    adjoint.astype(jnp.bfloat16),
                    (half_square[d, b] * adjoint).astype(jnp.bfloat16),
                ],
                axis=1,
            )
            both = jnp.concatenate([lin[b], quad[b]], axis=1)
            out = lax.dot_general(sent, both, TRANSPOSED, preferred_element_type=jnp.float32)
            for k in range(PICKS):
                contrib[b * PICKS + k] = out[:, k * LANES : (k + 1) * LANES]

    def add_up():
        running[0] = contrib[plan_ref[0]]

        @pl.loop(1, terms, unroll=UNROLL)
        def _(j):
            keep = plan_ref[terms + j].astype(jnp.float32)
            running[j] = contrib[plan_ref[j]] + keep * running[j - 1]

    def total(slot, h):
        p = slot * own + h
        used = plan_ref[2 * terms + fblocks + p].astype(jnp.float32)
        return running[plan_ref[2 * terms + p]] * used

    def core_copy(d, y, z):
        at = d, y * line + z
        return copy(core_out.at[at], core_in.at[at], core_send.at[at], core_recv.at[at], core_peer)

    def row_copy(d, z):
        at = d, z
        return copy(row_out.at[at], row_in.at[at], row_send.at[at], row_recv.at[at], row_peer)

    def line_copy(d, i, here, there):
        return copy(
            line_out.at[d, i], line_in.at[d, here], line_send.at[d, i], line_recv.at[d, here],
            index(there, row, core),
        )

    def core_stage(d):
        for y in (1 - row, row):
            @pl.loop(1, line + 1)
            def _(i):
                z = along(i)
                for h in range(own):
                    core_out[d, y * line + z, h] = total(index(z, y, 1 - core), h).astype(
                        jnp.bfloat16
                    )
                core_copy(d, y, z).start()

        for y in (1 - row, row):
            @pl.loop(0, line)
            def _(z):
                for h in range(own):
                    kept[d, y * line + z, h] = total(index(z, y, core), h)

    def row_part(d, i):
        z = along(i)
        core_copy(d, 1 - row, z).wait_recv()
        at = (1 - row) * line + z
        row_out[d, z] = (kept[d, at] + core_in[d, at].astype(jnp.float32)).astype(jnp.bfloat16)
        row_copy(d, z).start()

    def chip_sum(d, z):
        core_copy(d, row, z).wait_recv()
        row_copy(d, z).wait_recv()
        at = row * line + z
        return (
            kept[d, at]
            + core_in[d, at].astype(jnp.float32)
            + row_in[d, z].astype(jnp.float32)
        )

    def line_part(d, i):
        there = along(i)
        line_out[d, i] = chip_sum(d, there).astype(jnp.bfloat16)
        line_copy(d, i, place, there).start()

    def finish(d):
        found = chip_sum(d, place)
        for i in range(1, line):
            there = along(i)
            line_copy(d, i, there, there).wait_recv()
            found = found + line_in[d, there].astype(jnp.float32)
        for h in range(own):
            grad_ref[d, :, h * LANES : (h + 1) * LANES] = found[h] * (1.0 / norm_scale)

    exposure_part[...] = jnp.zeros_like(exposure_part)
    share = blocks // line
    forward(0, 0, share)
    for s in range(line - 2, line):
        row_step(1, s)
        forward(0, (s - line + 3) * share, (s - line + 4) * share)
    forward(0, 3 * share, blocks)
    exposure_send(0)
    core_steps(1)
    forward(1, 0, 2 * share)
    exposure_sum(0)
    forward(1, 2 * share, blocks)
    exposure_send(1)
    grad = exposure_grad(0)
    backward(0, grad, 0, 2 * share)
    exposure_sum(1)
    backward(0, grad, 2 * share, blocks)
    add_up()
    core_stage(0)
    grad = exposure_grad(1)
    backward(1, grad, 0, share)
    for i in range(1, line + 1):
        row_part(0, i)
    backward(1, grad, share, blocks)
    add_up()
    core_stage(1)
    for i in range(1, line):
        line_part(0, i)
        row_part(1, i)
    row_part(1, line)
    for i in range(1, line):
        line_part(1, i)
    for d in range(dates):
        finish(d)

    for d in range(dates):
        for z in range(line):
            @pl.when(goes_right(z))
            def _():
                to_right(d, z).wait_send()

            @pl.when(goes_left(z))
            def _():
                to_left(d, z).wait_send()

            to_row(d, z).wait_send()
            to_core(d, z, row, 3 * line).wait_send()
            to_core(d, z, 1 - row, 4 * line).wait_send()
        others(lambda t: piece_copy(d, t, me).wait_send())
        others(lambda t: full_copy(d, t, me).wait_send())
        for z in range(line):
            for y in range(ROWS):
                core_copy(d, y, z).wait_send()
            row_copy(d, z).wait_send()
        for i in range(1, line):
            line_copy(d, i, place, along(i)).wait_send()


def per_device_fused(
    panels,
    lin_weight,
    quad_weight,
    positions,
    pattern,
    netting,
    default_curve,
    date_ids,
    loss_given,
):
    size = lax.axis_size("trade")
    line = size // (CORES * ROWS)
    blocks, width = positions.shape
    dates, scen, columns = panels.shape
    own = columns // width
    fblocks = own * size
    terms = blocks * PICKS
    norm_scale = (NETS / (blocks * width * size)) ** 0.5
    flat = pattern.reshape(-1)
    at = jnp.arange(terms, dtype=jnp.int32)
    ahead = (flat[None, :] < flat[:, None]) | (
        (flat[None, :] == flat[:, None]) & (at[None, :] < at[:, None])
    )
    rank = jnp.sum(ahead, axis=1, dtype=jnp.int32)
    order = jnp.sum(jnp.where(rank[None, :] == at[:, None], at[None, :], 0), axis=1)
    ids = jnp.arange(fblocks, dtype=jnp.int32)
    first = jnp.sum(flat[None, :] < ids[:, None], axis=1, dtype=jnp.int32)
    count = jnp.sum(flat[None, :] == ids[:, None], axis=1, dtype=jnp.int32)
    last = jnp.maximum(first + count - 1, 0)
    used = jnp.minimum(count, 1)
    keep = 1 - jnp.max((first[None, :] == at[:, None]).astype(jnp.int32), axis=1)
    plan = jnp.concatenate([order, keep, last, used])

    smem = pl.BlockSpec(memory_space=pltpu.SMEM)
    vmem = pl.BlockSpec(memory_space=pltpu.VMEM)
    hbm = pl.BlockSpec(memory_space=pl.ANY)
    tile = (scen, width)
    f32, bf16 = jnp.float32, jnp.bfloat16
    dma = pltpu.SemaphoreType.DMA
    charge, panel_grad = pl.pallas_call(
        functools.partial(fused_kernel, size, line, norm_scale),
        out_shape=(
            jax.ShapeDtypeStruct((dates,), f32),
            jax.ShapeDtypeStruct((dates, scen, columns), f32),
        ),
        in_specs=[smem] * 5 + [vmem] * 3 + [hbm] * 2,
        out_specs=(smem, vmem),
        scratch_shapes=[
            pltpu.VMEM((blocks, PICKS * width, width), bf16),
            pltpu.VMEM((blocks, PICKS * width, width), bf16),
            pltpu.VMEM((fblocks,) + tile, bf16),
            pltpu.VMEM((fblocks,) + tile, bf16),
            pltpu.VMEM((dates, blocks) + tile, f32),
            pltpu.VMEM((dates, blocks) + tile, f32),
            pltpu.VMEM((dates, scen, NETS), f32),
            pltpu.VMEM((dates, size, scen // size, NETS), f32),
            pltpu.VMEM((dates, scen, NETS), f32),
            pltpu.VMEM((terms,) + tile, f32),
            pltpu.VMEM((terms,) + tile, f32),
            pltpu.VMEM((dates, ROWS * line, own) + tile, bf16),
            pltpu.VMEM((dates, ROWS * line, own) + tile, bf16),
            pltpu.VMEM((dates, ROWS * line, own) + tile, f32),
            pltpu.VMEM((dates, line, own) + tile, bf16),
            pltpu.VMEM((dates, line, own) + tile, bf16),
            pltpu.VMEM((dates, line, own) + tile, bf16),
            pltpu.VMEM((dates, line, own) + tile, bf16),
            dma((2,)),
            dma((dates, 5 * line)),
            dma((dates, size)),
            dma((dates, size)),
            dma((dates, size)),
            dma((dates, size)),
            dma((dates, size)),
            dma((dates, ROWS * line)),
            dma((dates, ROWS * line)),
            dma((dates, line)),
            dma((dates, line)),
            dma((dates, line)),
            dma((dates, line)),
        ],
        compiler_params=pltpu.CompilerParams(
            collective_id=0, has_side_effects=True, vmem_limit_bytes=56 * 1024 * 1024
        ),
        name="fused",
    )(
        plan, flat, netting, date_ids, default_curve,
        panels, positions, loss_given.reshape(1, -1),
        lin_weight.reshape(blocks, PICKS * width, width),
        quad_weight.reshape(blocks, PICKS * width, width),
    )
    return (charge, panel_grad)


def fits_kernel(mesh, panels, positions, loss_given):
    size = mesh.shape["trade"]
    width = positions.shape[1]
    line = size // (CORES * ROWS)
    return (
        panels.shape[0] == 2
        and width == LANES
        and line * CORES * ROWS == size
        and line == 4
        and (panels.shape[2] // size) % width == 0
        and (panels.shape[1] // mesh.shape["parts"]) % (8 * size) == 0
    )


def solution(mesh):
    in_specs = (
        P(None, "parts", "trade"),
        P(("parts", "trade"), None, None, None),
        P(("parts", "trade"), None, None, None),
        P(("parts", "trade"), None),
        P(("parts", "trade"), None),
        P(("parts", "trade")),
        P(),
        P(),
        P("parts"),
    )
    out_specs = (P("parts"), P(None, "parts", "trade"))

    def run(*args):
        body = per_device_fused if fits_kernel(mesh, args[0], args[3], args[8]) else per_device
        return jax.shard_map(
            body, mesh=mesh, in_specs=in_specs, out_specs=out_specs, check_vma=False
        )(*args)

    return run
```

```python
import functools

import jax
import jax.numpy as jnp
from jax import lax
from jax.experimental import pallas as pl
from jax.experimental.pallas import tpu as pltpu
from jax.sharding import PartitionSpec as P

PICKS = 4
NETS = 128


def per_device(
    panels,
    lin_weight,
    quad_weight,
    positions,
    pattern,
    netting,
    default_curve,
    date_ids,
    loss_given,
):
    devices = lax.axis_size("trade")
    local_blocks, block_width = positions.shape
    trades_all = local_blocks * block_width * devices
    norm_scale = (NETS / trades_all) ** 0.5
    grad_unit = 1.0 / norm_scale
    factors = panels.shape[2] * devices
    fblocks = factors // block_width
    horizon = jnp.arange(default_curve.shape[0], dtype=jnp.int32)
    weights = jnp.sum(
        jnp.where(date_ids[:, None] == horizon[None, :], default_curve[None, :], 0.0), axis=1
    )
    set_map = (netting[:, None] == jnp.arange(NETS, dtype=jnp.int32)[None, :]).astype(jnp.float32)
    flat_pattern = pattern.reshape(-1)
    block_map = (flat_pattern[:, None] == jnp.arange(fblocks, dtype=jnp.int32)[None, :]).astype(
        jnp.float32
    )
    gathered = lax.all_gather(panels, "trade", axis=2, tiled=True)
    leading = gathered.shape[:-1]
    blocks = gathered.reshape(leading + (fblocks, block_width))
    picked = jnp.take(blocks, flat_pattern, axis=-2).reshape(
        leading + (local_blocks, PICKS, block_width)
    )
    linear = jnp.einsum(
        "...bkc,bkct->...bt", picked, lin_weight, preferred_element_type=jnp.float32
    )
    square_term = jnp.einsum(
        "...bkc,bkct->...bt", picked, quad_weight, preferred_element_type=jnp.float32
    )
    trade_state = linear + 0.25 * square_term * square_term
    block_sum = jnp.sum(positions * jax.nn.softplus(trade_state), axis=-1)
    local_exposure = norm_scale * jnp.einsum(
        "...b,bn->...n", block_sum, set_map, precision=lax.Precision.HIGHEST
    )
    local_exposure, square_term, trade_state = (local_exposure, square_term, trade_state)
    exposure = lax.psum(local_exposure, "trade")
    losses = jnp.sum(loss_given * jax.nn.softplus(exposure), axis=-1)
    charge = weights * jnp.mean(losses, axis=-1)
    exposure_grad = weights[:, None, None] * loss_given * jax.nn.sigmoid(exposure)
    block_adjoint = norm_scale * jnp.einsum(
        "...n,bn->...b", exposure_grad, set_map, precision=lax.Precision.HIGHEST
    )
    state_adjoint = block_adjoint[..., None] * positions * jax.nn.sigmoid(trade_state)
    adjoint_lin = state_adjoint.astype(jnp.bfloat16)
    adjoint_square = (0.5 * square_term * state_adjoint).astype(jnp.bfloat16)
    contrib = jnp.einsum(
        "...bt,bkct->...bkc", adjoint_lin, lin_weight, preferred_element_type=jnp.float32
    )
    contrib = contrib + jnp.einsum(
        "...bt,bkct->...bkc", adjoint_square, quad_weight, preferred_element_type=jnp.float32
    )
    leading = contrib.shape[:-3]
    flat_contrib = contrib.reshape(leading + (local_blocks * PICKS, block_width))
    leading = flat_contrib.shape[:-2]
    placed = jnp.einsum("...jc,jf->...fc", flat_contrib, block_map, precision=lax.Precision.HIGHEST)
    panel_grad = lax.psum_scatter(
        (grad_unit * placed).reshape(leading + (factors,)), "trade", scatter_dimension=2, tiled=True
    )
    return (charge, panel_grad)


MESH = pl.DeviceIdType.MESH
LANES = 128
CORES = 2
ROWS = 2
UNROLL = 8
TRANSPOSED = (((1,), (1,)), ((), ()))


def fused_kernel(
    size,
    line,
    norm_scale,
    plan_ref,
    pattern_ref,
    netting_ref,
    dates_ref,
    curve_ref,
    panels_ref,
    positions_ref,
    loss_ref,
    lin_hbm,
    quad_hbm,
    charge_ref,
    grad_ref,
    lin,
    quad,
    panels_a,
    panels_b,
    slope,
    half_square,
    exposure_part,
    exposure_pieces,
    exposure_full,
    contrib,
    running,
    core_out,
    core_in,
    kept,
    row_out,
    row_in,
    line_out,
    line_in,
    weight_sem,
    gather_send,
    gather_recv,
    piece_send,
    piece_recv,
    full_send,
    full_recv,
    core_send,
    core_recv,
    row_send,
    row_recv,
    line_send,
    line_recv,
):
    me = lax.axis_index("trade")
    core = lax.rem(me, CORES)
    row = lax.rem(me // CORES, ROWS)
    place = me // (CORES * ROWS)
    blocks = positions_ref.shape[0]
    scen = panels_ref.shape[1]
    own = panels_ref.shape[2] // LANES
    piece = scen // size
    terms = blocks * PICKS
    fblocks = own * size
    gathered = (panels_a, panels_b)
    dates = len(gathered)

    def index(z, y, c):
        return (z * ROWS + y) * CORES + c

    def along(i):
        return lax.rem(place + i, line)

    def copy(src, dst, send, recv, peer):
        return pltpu.make_async_remote_copy(
            src_ref=src, dst_ref=dst, send_sem=send, recv_sem=recv,
            device_id={"trade": peer}, device_id_type=MESH,
        )

    row_peer = index(place, 1 - row, core)
    core_peer = index(place, row, 1 - core)

    weight_copies = [
        pltpu.make_async_copy(lin_hbm, lin, weight_sem.at[0]),
        pltpu.make_async_copy(quad_hbm, quad, weight_sem.at[1]),
    ]
    for each in weight_copies:
        each.start()

    for d in range(dates):
        for h in range(own):
            gathered[d][me * own + h] = panels_ref[d, :, h * LANES : (h + 1) * LANES]

    barrier = pltpu.get_barrier_semaphore()

    @pl.loop(1, size)
    def _(i):
        pl.semaphore_signal(
            barrier, inc=1, device_id={"trade": lax.rem(me + i, size)}, device_id_type=MESH
        )

    pl.semaphore_wait(barrier, size - 1)

    def panel_copy(d, slot, peer, k):
        part = gathered[d].at[pl.ds(slot * own, own)]
        return copy(part, part, gather_send.at[d, k], gather_recv.at[d, slot], peer)

    def to_right(d, z):
        return panel_copy(d, index(z, row, core), index(place + 1, row, core), z)

    def to_left(d, z):
        return panel_copy(d, index(z, row, core), index(place - 1, row, core), line + z)

    def to_row(d, z):
        return panel_copy(d, index(z, row, core), row_peer, 2 * line + z)

    def to_core(d, z, y, k):
        return panel_copy(d, index(z, y, core), core_peer, k + z)

    def panel_wait(d, slot):
        panel_copy(d, slot, core_peer, 0).wait_recv()

    def goes_right(z):
        return jnp.logical_and(z <= place, place < line - 1)

    def goes_left(z):
        return jnp.logical_and(z >= place, place > 0)

    def pass_on(d, z):
        @pl.when(goes_right(z))
        def _():
            to_right(d, z).start()

        @pl.when(goes_left(z))
        def _():
            to_left(d, z).start()

        to_row(d, z).start()
        to_core(d, z, row, 3 * line).start()

    def both_sides(s, act):
        @pl.when(place >= s)
        def _():
            act(place - s)

        if s > 0:
            @pl.when(place + s < line)
            def _():
                act(place + s)

    def line_step(d, s):
        def act(z):
            panel_wait(d, index(z, row, core))
            pass_on(d, z)

        both_sides(s, act)

    def row_step(d, s):
        def act(z):
            panel_wait(d, index(z, 1 - row, core))
            to_core(d, z, 1 - row, 4 * line).start()

        both_sides(s, act)

    def core_steps(d):
        for z in range(line):
            for y in range(ROWS):
                panel_wait(d, index(z, y, 1 - core))

    pass_on(0, place)
    pass_on(1, place)
    line_step(0, 1)
    row_step(0, 0)
    for s in range(2, line):
        line_step(1, s - 1)
        line_step(0, s)
        row_step(1, s - 2)
        row_step(0, s - 1)
    line_step(1, line - 1)
    row_step(0, line - 1)
    core_steps(0)
    for each in weight_copies:
        each.wait()

    lane = lax.broadcasted_iota(jnp.int32, (1, LANES), 1)

    def forward(d, first, stop):
        @pl.loop(first, stop, unroll=UNROLL)
        def _(b):
            picked = jnp.concatenate(
                [gathered[d][pattern_ref[b * PICKS + k]] for k in range(PICKS)], axis=1
            )
            both = jnp.concatenate([lin[b], quad[b]], axis=1)
            terms = jnp.dot(picked, both, preferred_element_type=jnp.float32)
            square = terms[:, LANES:]
            state = terms[:, :LANES] + 0.25 * square * square
            small = jnp.exp(-jnp.abs(state))
            above = 1.0 + small
            soft = jnp.maximum(state, 0.0) + jnp.log(above)
            sigmoid = jnp.where(state >= 0.0, 1.0, small) / above
            held = positions_ref[pl.ds(b, 1), :]
            block_sum = jnp.sum(held * soft, axis=1, keepdims=True)
            in_set = jnp.where(lane == netting_ref[b], norm_scale, 0.0)
            exposure_part[d] += block_sum * in_set
            slope[d, b] = held * sigmoid
            half_square[d, b] = 0.5 * square

    def piece_rows(t):
        return pl.ds(pl.multiple_of(t * piece, piece), piece)

    def piece_copy(d, t, source):
        return copy(
            exposure_part.at[d, piece_rows(t)], exposure_pieces.at[d, source],
            piece_send.at[d, t], piece_recv.at[d, source], t,
        )

    def full_copy(d, t, source):
        return copy(
            exposure_full.at[d, piece_rows(source)], exposure_full.at[d, piece_rows(source)],
            full_send.at[d, t], full_recv.at[d, source], t,
        )

    def others(act):
        @pl.loop(1, size, unroll=5)
        def _(i):
            act(lax.rem(me + i, size))

    def exposure_send(d):
        exposure_pieces[d, me] = exposure_part[d, piece_rows(me), :]
        others(lambda t: piece_copy(d, t, me).start())

    def exposure_sum(d):
        others(lambda t: piece_copy(d, t, t).wait_recv())
        exposure_full[d, piece_rows(me), :] = jnp.sum(exposure_pieces[d], axis=0)
        others(lambda t: full_copy(d, t, me).start())

    def exposure_grad(d):
        others(lambda t: full_copy(d, t, t).wait_recv())
        exposure = exposure_full[d]
        small = jnp.exp(-jnp.abs(exposure))
        above = 1.0 + small
        loss = loss_ref[...]
        weight = curve_ref[dates_ref[d]]
        soft = jnp.maximum(exposure, 0.0) + jnp.log(above)
        charge_ref[d] = weight * (jnp.sum(loss * soft) * (1.0 / scen))
        return weight * loss * (jnp.where(exposure >= 0.0, 1.0, small) / above)

    def backward(d, grad, first, stop):
        @pl.loop(first, stop, unroll=UNROLL)
        def _(b):
            in_set = jnp.where(lane == netting_ref[b], norm_scale, 0.0)
            adjoint = jnp.sum(grad * in_set, axis=1, keepdims=True) * slope[d, b]
            sent = jnp.concatenate(
                [
                    adjoint.astype(jnp.bfloat16),
                    (half_square[d, b] * adjoint).astype(jnp.bfloat16),
                ],
                axis=1,
            )
            both = jnp.concatenate([lin[b], quad[b]], axis=1)
            out = lax.dot_general(sent, both, TRANSPOSED, preferred_element_type=jnp.float32)
            for k in range(PICKS):
                contrib[b * PICKS + k] = out[:, k * LANES : (k + 1) * LANES]

    def add_up():
        running[0] = contrib[plan_ref[0]]

        @pl.loop(1, terms, unroll=UNROLL)
        def _(j):
            keep = plan_ref[terms + j].astype(jnp.float32)
            running[j] = contrib[plan_ref[j]] + keep * running[j - 1]

    def total(slot, h):
        p = slot * own + h
        used = plan_ref[2 * terms + fblocks + p].astype(jnp.float32)
        return running[plan_ref[2 * terms + p]] * used

    def core_copy(d, y, z):
        at = d, y * line + z
        return copy(core_out.at[at], core_in.at[at], core_send.at[at], core_recv.at[at], core_peer)

    def row_copy(d, z):
        at = d, z
        return copy(row_out.at[at], row_in.at[at], row_send.at[at], row_recv.at[at], row_peer)

    def line_copy(d, i, here, there):
        return copy(
            line_out.at[d, i], line_in.at[d, here], line_send.at[d, i], line_recv.at[d, here],
            index(there, row, core),
        )

    def core_stage(d):
        for y in (1 - row, row):
            @pl.loop(1, line + 1, unroll=line)
            def _(i):
                z = along(i)
                for h in range(own):
                    core_out[d, y * line + z, h] = total(index(z, y, 1 - core), h).astype(
                        jnp.bfloat16
                    )
                core_copy(d, y, z).start()

        for y in (1 - row, row):
            @pl.loop(0, line, unroll=line)
            def _(z):
                for h in range(own):
                    kept[d, y * line + z, h] = total(index(z, y, core), h)

    def row_part(d, i):
        z = along(i)
        core_copy(d, 1 - row, z).wait_recv()
        at = (1 - row) * line + z
        row_out[d, z] = (kept[d, at] + core_in[d, at].astype(jnp.float32)).astype(jnp.bfloat16)
        row_copy(d, z).start()

    def chip_sum(d, z):
        core_copy(d, row, z).wait_recv()
        row_copy(d, z).wait_recv()
        at = row * line + z
        return (
            kept[d, at]
            + core_in[d, at].astype(jnp.float32)
            + row_in[d, z].astype(jnp.float32)
        )

    def line_part(d, i):
        there = along(i)
        line_out[d, i] = chip_sum(d, there).astype(jnp.bfloat16)
        line_copy(d, i, place, there).start()

    def finish(d):
        found = chip_sum(d, place)
        for i in range(1, line):
            there = along(i)
            line_copy(d, i, there, there).wait_recv()
            found = found + line_in[d, there].astype(jnp.float32)
        for h in range(own):
            grad_ref[d, :, h * LANES : (h + 1) * LANES] = found[h] * (1.0 / norm_scale)

    exposure_part[...] = jnp.zeros_like(exposure_part)
    share = blocks // line
    forward(0, 0, share)
    for s in range(line - 2, line):
        row_step(1, s)
        forward(0, (s - line + 3) * share, (s - line + 4) * share)
    forward(0, 3 * share, blocks)
    exposure_send(0)
    core_steps(1)
    forward(1, 0, 2 * share)
    exposure_sum(0)
    forward(1, 2 * share, blocks)
    exposure_send(1)
    grad = exposure_grad(0)
    backward(0, grad, 0, 2 * share)
    exposure_sum(1)
    backward(0, grad, 2 * share, blocks)
    add_up()
    core_stage(0)
    grad = exposure_grad(1)
    backward(1, grad, 0, share)
    for i in range(1, line + 1):
        row_part(0, i)
    backward(1, grad, share, blocks)
    add_up()
    core_stage(1)
    for i in range(1, line):
        line_part(0, i)
        row_part(1, i)
    row_part(1, line)
    for i in range(1, line):
        line_part(1, i)
    for d in range(dates):
        finish(d)

    for d in range(dates):
        for z in range(line):
            @pl.when(goes_right(z))
            def _():
                to_right(d, z).wait_send()

            @pl.when(goes_left(z))
            def _():
                to_left(d, z).wait_send()

            to_row(d, z).wait_send()
            to_core(d, z, row, 3 * line).wait_send()
            to_core(d, z, 1 - row, 4 * line).wait_send()
        others(lambda t: piece_copy(d, t, me).wait_send())
        others(lambda t: full_copy(d, t, me).wait_send())
        for z in range(line):
            for y in range(ROWS):
                core_copy(d, y, z).wait_send()
            row_copy(d, z).wait_send()
        for i in range(1, line):
            line_copy(d, i, place, along(i)).wait_send()


def per_device_fused(
    panels,
    lin_weight,
    quad_weight,
    positions,
    pattern,
    netting,
    default_curve,
    date_ids,
    loss_given,
):
    size = lax.axis_size("trade")
    line = size // (CORES * ROWS)
    blocks, width = positions.shape
    dates, scen, columns = panels.shape
    own = columns // width
    fblocks = own * size
    terms = blocks * PICKS
    norm_scale = (NETS / (blocks * width * size)) ** 0.5
    flat = pattern.reshape(-1)
    at = jnp.arange(terms, dtype=jnp.int32)
    ahead = (flat[None, :] < flat[:, None]) | (
        (flat[None, :] == flat[:, None]) & (at[None, :] < at[:, None])
    )
    rank = jnp.sum(ahead, axis=1, dtype=jnp.int32)
    order = jnp.sum(jnp.where(rank[None, :] == at[:, None], at[None, :], 0), axis=1)
    ids = jnp.arange(fblocks, dtype=jnp.int32)
    first = jnp.sum(flat[None, :] < ids[:, None], axis=1, dtype=jnp.int32)
    count = jnp.sum(flat[None, :] == ids[:, None], axis=1, dtype=jnp.int32)
    last = jnp.maximum(first + count - 1, 0)
    used = jnp.minimum(count, 1)
    keep = 1 - jnp.max((first[None, :] == at[:, None]).astype(jnp.int32), axis=1)
    plan = jnp.concatenate([order, keep, last, used])

    smem = pl.BlockSpec(memory_space=pltpu.SMEM)
    vmem = pl.BlockSpec(memory_space=pltpu.VMEM)
    hbm = pl.BlockSpec(memory_space=pl.ANY)
    tile = (scen, width)
    f32, bf16 = jnp.float32, jnp.bfloat16
    dma = pltpu.SemaphoreType.DMA
    charge, panel_grad = pl.pallas_call(
        functools.partial(fused_kernel, size, line, norm_scale),
        out_shape=(
            jax.ShapeDtypeStruct((dates,), f32),
            jax.ShapeDtypeStruct((dates, scen, columns), f32),
        ),
        in_specs=[smem] * 5 + [vmem] * 3 + [hbm] * 2,
        out_specs=(smem, vmem),
        scratch_shapes=[
            pltpu.VMEM((blocks, PICKS * width, width), bf16),
            pltpu.VMEM((blocks, PICKS * width, width), bf16),
            pltpu.VMEM((fblocks,) + tile, bf16),
            pltpu.VMEM((fblocks,) + tile, bf16),
            pltpu.VMEM((dates, blocks) + tile, f32),
            pltpu.VMEM((dates, blocks) + tile, f32),
            pltpu.VMEM((dates, scen, NETS), f32),
            pltpu.VMEM((dates, size, scen // size, NETS), f32),
            pltpu.VMEM((dates, scen, NETS), f32),
            pltpu.VMEM((terms,) + tile, f32),
            pltpu.VMEM((terms,) + tile, f32),
            pltpu.VMEM((dates, ROWS * line, own) + tile, bf16),
            pltpu.VMEM((dates, ROWS * line, own) + tile, bf16),
            pltpu.VMEM((dates, ROWS * line, own) + tile, f32),
            pltpu.VMEM((dates, line, own) + tile, bf16),
            pltpu.VMEM((dates, line, own) + tile, bf16),
            pltpu.VMEM((dates, line, own) + tile, bf16),
            pltpu.VMEM((dates, line, own) + tile, bf16),
            dma((2,)),
            dma((dates, 5 * line)),
            dma((dates, size)),
            dma((dates, size)),
            dma((dates, size)),
            dma((dates, size)),
            dma((dates, size)),
            dma((dates, ROWS * line)),
            dma((dates, ROWS * line)),
            dma((dates, line)),
            dma((dates, line)),
            dma((dates, line)),
            dma((dates, line)),
        ],
        compiler_params=pltpu.CompilerParams(
            collective_id=0, has_side_effects=True, vmem_limit_bytes=56 * 1024 * 1024
        ),
        name="fused",
    )(
        plan, flat, netting, date_ids, default_curve,
        panels, positions, loss_given.reshape(1, -1),
        lin_weight.reshape(blocks, PICKS * width, width),
        quad_weight.reshape(blocks, PICKS * width, width),
    )
    return (charge, panel_grad)


def fits_kernel(mesh, panels, positions, loss_given):
    size = mesh.shape["trade"]
    width = positions.shape[1]
    line = size // (CORES * ROWS)
    return (
        panels.shape[0] == 2
        and width == LANES
        and line * CORES * ROWS == size
        and line == 4
        and (panels.shape[2] // size) % width == 0
        and (panels.shape[1] // mesh.shape["parts"]) % (8 * size) == 0
    )


def solution(mesh):
    in_specs = (
        P(None, "parts", "trade"),
        P(("parts", "trade"), None, None, None),
        P(("parts", "trade"), None, None, None),
        P(("parts", "trade"), None),
        P(("parts", "trade"), None),
        P(("parts", "trade")),
        P(),
        P(),
        P("parts"),
    )
    out_specs = (P("parts"), P(None, "parts", "trade"))

    def run(*args):
        body = per_device_fused if fits_kernel(mesh, args[0], args[3], args[8]) else per_device
        return jax.shard_map(
            body, mesh=mesh, in_specs=in_specs, out_specs=out_specs, check_vma=False
        )(*args)

    return run
```
